32 devices in a mesh: dp: 16 (over z, y, x), branch: 2 (over core).
Axes of the slice: x: 2, y: 2, z: 4, core: 2. Of those that a mesh axis runs over, the one named last changes fastest.
Arguments:
- node_states: bfloat16 [32768, 256], P(('dp', 'branch'))
- cotangent: bfloat16 [32768, 256], P(('dp', 'branch')), may hold values from -6 to 6
- counts: int32 [512], P('dp'), may hold values from 3 to 51, as said below
- bond_types: int32 [512, 64, 64], P('dp'), may hold values from 0 to 5, as said below
- edge_table: float32 [5, 256], replicated, may hold values from -3 to 3
- gine_weight_one: bfloat16 [256, 256], replicated, may hold values from -0.375 to 0.375
- gine_bias_one: float32 [256], replicated, may hold values from -2 to 2
- gine_weight_two: bfloat16 [256, 256], replicated, may hold values from -0.375 to 0.375
- gine_gain: float32 [256], replicated, may hold values from 0.5 to 1.5
- gine_shift: float32 [256], replicated, may hold values from -2 to 2
- query_weight: bfloat16 [256, 256], replicated, may hold values from -0.375 to 0.375
- query_bias: float32 [256], replicated, may hold values from -2 to 2
- key_weight: bfloat16 [256, 256], replicated, may hold values from -0.375 to 0.375
- value_weight: bfloat16 [256, 256], replicated, may hold values from -0.375 to 0.375
- out_weight: bfloat16 [256, 256], replicated, may hold values from -1 to 1
- attn_gain: float32 [256], replicated, may hold values from 0.5 to 1.5
- attn_shift: float32 [256], replicated, may hold values from -2 to 2
- ffn_weight_up: bfloat16 [256, 512], replicated, may hold values from -0.375 to 0.375
- ffn_bias_up: float32 [512], replicated, may hold values from -2 to 2
- ffn_weight_down: bfloat16 [512, 256], replicated, may hold values from -0.25 to 0.25
- final_gain: float32 [256], replicated, may hold values from 0.5 to 1.5
- final_shift: float32 [256], replicated, may hold values from -2 to 2
Outputs:
- layer_output: bfloat16 [32768, 256], P(('dp', 'branch'))
- node_grads: float32 [32768, 256], P(('dp', 'branch'))
- edge_table_grad: float32 [5, 256], replicated
- gine_weight_one_grad: float32 [256, 256], replicated
- gine_bias_one_grad: float32 [256], replicated
- gine_weight_two_grad: float32 [256, 256], replicated
- gine_gain_grad: float32 [256], replicated
- gine_shift_grad: float32 [256], replicated
- query_weight_grad: float32 [256, 256], replicated
- query_bias_grad: float32 [256], replicated
- key_weight_grad: float32 [256, 256], replicated
- value_weight_grad: float32 [256, 256], replicated
- out_weight_grad: float32 [256, 256], replicated
- attn_gain_grad: float32 [256], replicated
- attn_shift_grad: float32 [256], replicated
- ffn_weight_up_grad: float32 [256, 512], replicated
- ffn_bias_up_grad: float32 [512], replicated
- ffn_weight_down_grad: float32 [512, 256], replicated
- final_gain_grad: float32 [256], replicated
- final_shift_grad: float32 [256], replicated
The draws below stay inside these ranges and needn't reach their ends.
Inputs may be any that keep to these rules, and one draw needn't show every extreme that they name: `counts`: nodes of each molecule; some molecule has exactly 51 nodes and some exactly 3. `bond_types`: symmetric, 0 on the diagonal and wherever a slot is not below its molecule's count; every molecule's consecutive nodes are bonded.
All inputs are finite; a program needn't handle non-finite values.
Results may differ from the reference program's by a relative error of at most 0.023.
Values may be sent and summed in bfloat16 or wider, within the bound.
A program may use at most 128 MiB of HBM per device.

```python
import math
import jax
import jax.numpy as jnp
from jax import lax

D = 256
HEADS = 8
FF = 512
ET = 5
SLOT = 64
MOST = 51
TOTAL_GRAPHS = 512
NODES = 32768


def shared_counts(key):
    first_draw = jax.random.randint(jax.random.fold_in(key, 11), (TOTAL_GRAPHS,), 3, MOST + 1)
    second_draw = jax.random.randint(jax.random.fold_in(key, 12), (TOTAL_GRAPHS,), 3, MOST + 1)
    sizes = jnp.maximum(first_draw, second_draw)
    sizes = sizes.at[0].set(MOST).at[1].set(3)
    return sizes.astype(jnp.int32)


def draw_counts(key, part):
    sizes = shared_counts(key)
    return sizes


def draw_bond_types(key, part):
    sizes = shared_counts(key)
    key = jax.random.fold_in(key, 5)
    pick_key, kind_key = jax.random.split(key)
    places = jnp.arange(SLOT)
    chance = jax.random.randint(pick_key, (TOTAL_GRAPHS, SLOT, SLOT), 0, 100)
    chance = jnp.minimum(chance, jnp.swapaxes(chance, 1, 2))
    kinds = jax.random.randint(kind_key, (TOTAL_GRAPHS, SLOT, SLOT), 1, ET + 1)
    upper = places[:, None] < places[None, :]
    kinds = jnp.where(upper[None], kinds, jnp.swapaxes(kinds, 1, 2))
    spacing = jnp.abs(places[:, None] - places[None, :])
    linked = (spacing == 1)[None] | (chance < 3) & (spacing > 1)[None]
    inside = (places[None, :, None] < sizes[:, None, None]) & (places[None, None, :] < sizes[:, None, None])
    return jnp.where(linked & inside, kinds, 0).astype(jnp.int32)


def draw_node_states(key, part):
    key = jax.random.fold_in(key, 7)
    position = (jnp.arange(NODES, dtype=jnp.float32) / NODES)[:, None]
    noise = jax.random.normal(key, (NODES, D), jnp.float32)
    return (noise * (0.6 + 1.2 * position) + 0.5 * position).astype(jnp.bfloat16)


def level_of(own_key, dims, pieces, least, high):
    level, own = 1.0, jax.random.fold_in(own_key, 6)
    for dim, shards_of in pieces:
        steps = jnp.exp(jax.random.uniform(jax.random.fold_in(own, dim), (shards_of,), jnp.float32, least / len(pieces), high / len(pieces)))
        level = level * jnp.repeat(steps, dims[dim] // shards_of).reshape([-1 if axis == dim else 1 for axis in range(len(dims))])
    return level


def scatter_about(stream_key, extent, width, bound, shards=(), kind=jnp.bfloat16):
    factor_of = level_of(stream_key, extent, shards, -0.22, 0.18) if shards else 1.0
    drawn = jax.random.normal(stream_key, extent, jnp.float32) * width * factor_of
    return jnp.minimum(jnp.maximum(drawn, -bound), bound).astype(kind)


def setup_inputs(seed: int = 0) -> dict:
    key_of = jax.random.split(jax.random.key(seed), 23)
    node_states = draw_node_states(jax.random.fold_in(key_of[22], 71), 0)
    cotangent = scatter_about(key_of[1], (NODES, D), 1.0, 6.0, ((0, 32),))
    counts = draw_counts(jax.random.fold_in(key_of[22], 71), 0)
    bond_types = draw_bond_types(jax.random.fold_in(key_of[22], 71), 0)
    edge_table = scatter_about(key_of[4], (ET, D), 0.5, 3.0, (), jnp.float32)
    gine_weight_one = scatter_about(key_of[5], (D, D), D ** -0.5, 0.375)
    gine_bias_one = scatter_about(key_of[6], (D,), 0.3, 2.0, (), jnp.float32)
    gine_weight_two = scatter_about(key_of[7], (D, D), D ** -0.5, 0.375)
    gine_gain = jnp.clip(1.0 + 0.1 * jax.random.normal(key_of[8], (D,), jnp.float32), 0.5, 1.5)
    gine_shift = scatter_about(key_of[9], (D,), 0.3, 2.0, (), jnp.float32)
    query_weight = scatter_about(key_of[10], (D, D), D ** -0.5, 0.375)
    query_bias = scatter_about(key_of[11], (D,), 0.3, 2.0, (), jnp.float32)
    key_weight = scatter_about(key_of[12], (D, D), D ** -0.5, 0.375)
    value_weight = scatter_about(key_of[13], (D, D), D ** -0.5, 0.375)
    out_weight = scatter_about(key_of[14], (D, D), (D // 8) ** -0.5, 1.0)
    attn_gain = jnp.clip(1.0 + 0.1 * jax.random.normal(key_of[15], (D,), jnp.float32), 0.5, 1.5)
    attn_shift = scatter_about(key_of[16], (D,), 0.3, 2.0, (), jnp.float32)
    ffn_weight_up = scatter_about(key_of[17], (D, FF), D ** -0.5, 0.375)
    ffn_bias_up = scatter_about(key_of[18], (FF,), 0.3, 2.0, (), jnp.float32)
    ffn_weight_down = scatter_about(key_of[19], (FF, D), FF ** -0.5, 0.25)
    final_gain = jnp.clip(1.0 + 0.1 * jax.random.normal(key_of[20], (D,), jnp.float32), 0.5, 1.5)
    final_shift = scatter_about(key_of[21], (D,), 0.3, 2.0, (), jnp.float32)
    return {"node_states": node_states, "cotangent": cotangent, "counts": counts, "bond_types": bond_types, "edge_table": edge_table, "gine_weight_one": gine_weight_one, "gine_bias_one": gine_bias_one, "gine_weight_two": gine_weight_two, "gine_gain": gine_gain, "gine_shift": gine_shift, "query_weight": query_weight, "query_bias": query_bias, "key_weight": key_weight, "value_weight": value_weight, "out_weight": out_weight, "attn_gain": attn_gain, "attn_shift": attn_shift, "ffn_weight_up": ffn_weight_up, "ffn_bias_up": ffn_bias_up, "ffn_weight_down": ffn_weight_down, "final_gain": final_gain, "final_shift": final_shift}


@jax.custom_vjp
def low(v):
    return lax.optimization_barrier(v.astype(jnp.bfloat16)).astype(jnp.float32)

@jax.custom_vjp
def low_back(v):
    return v

def low_keep(v):
    return (low(v), None)

def low_pass(kept, grad):
    return (grad,)

def back_keep(v):
    return (v, None)

def back_low(kept, grad):
    return (low(grad),)
low.defvjp(low_keep, low_pass)
low_back.defvjp(back_keep, back_low)
epsilon = 1e-05
masked_score = -1e+30

def matmul_high(left, right):
    return jnp.dot(left, right, precision=lax.Precision.HIGHEST)

def batch_norm(values, present, node_total, gain, shift):
    centre = lax.optimization_barrier(jnp.sum(present * values, axis=0)) / node_total
    offset = values - centre
    spread = lax.optimization_barrier(jnp.sum(present * offset * offset, axis=0)) / node_total
    return present * (gain * offset * lax.rsqrt(spread + epsilon) + shift)

def reference(node_states, cotangent, counts, bond_types, edge_table, gine_weight_one, gine_bias_one, gine_weight_two, gine_gain, gine_shift, query_weight, query_bias, key_weight, value_weight, out_weight, attn_gain, attn_shift, ffn_weight_up, ffn_bias_up, ffn_weight_down, final_gain, final_shift):
    graphs = counts.shape[0]
    present = (jnp.arange(SLOT)[None, :] < counts[:, None]).reshape(-1).astype(jnp.float32)[:, None]
    node_total = jnp.sum(present)
    live_keys = present.reshape(graphs, 1, 1, SLOT) > 0.5
    onehot = (bond_types[None] == (1 + jnp.arange(ET))[:, None, None, None]).astype(jnp.float32)
    head_size = D // HEADS
    scaling = 1.0 / math.sqrt(head_size)

    def forward(states, table, weight_one, bias_one, weight_two, g_gain, g_shift, q_weight, q_bias, k_weight, v_weight, o_weight, a_gain, a_shift, up_weight, up_bias, down_weight, f_gain, f_shift):
        shifted = states[None] + table[:, None, :]
        sent = low(jax.nn.silu(shifted))
        message = low_back(jnp.einsum('tgij,tgjd->gid', onehot, sent.reshape(ET, graphs, SLOT, D), precision=lax.Precision.HIGHEST).reshape(-1, D))
        joined = low(states + message)
        gine_first = low_back(matmul_high(joined, weight_one) + bias_one)
        gine_last = low_back(matmul_high(low(jax.nn.silu(gine_first)), weight_two))
        local_out = batch_norm(gine_last + states, present, node_total, g_gain, g_shift)
        query = low_back(low(matmul_high(states, q_weight) + q_bias)).reshape(graphs, SLOT, HEADS, head_size)
        keys = low_back(low(matmul_high(states, k_weight))).reshape(graphs, SLOT, HEADS, head_size)
        values = low_back(low(matmul_high(states, v_weight))).reshape(graphs, SLOT, HEADS, head_size)
        scores = jnp.einsum('gihe,gjhe->ghij', query, keys, precision=lax.Precision.HIGHEST) * scaling
        scores = low_back(jnp.where(live_keys, scores, masked_score))
        probs = jax.nn.softmax(scores, axis=-1)
        mixed = low_back(low(jnp.einsum('ghij,gjhe->gihe', low(probs), values, precision=lax.Precision.HIGHEST).reshape(-1, D)))
        attn_out = low_back(matmul_high(mixed, o_weight))
        global_out = batch_norm(attn_out + states, present, node_total, a_gain, a_shift)
        joined_h = low_back(local_out + global_out)
        up_pre = low_back(matmul_high(low(joined_h), up_weight) + up_bias)
        down_pre = low_back(matmul_high(low(jax.nn.silu(up_pre)), down_weight))
        return batch_norm(joined_h + down_pre, present, node_total, f_gain, f_shift)
    inputs = (node_states.astype(jnp.float32), edge_table, gine_weight_one.astype(jnp.float32), gine_bias_one, gine_weight_two.astype(jnp.float32), gine_gain, gine_shift, query_weight.astype(jnp.float32), query_bias, key_weight.astype(jnp.float32), value_weight.astype(jnp.float32), out_weight.astype(jnp.float32), attn_gain, attn_shift, ffn_weight_up.astype(jnp.float32), ffn_bias_up, ffn_weight_down.astype(jnp.float32), final_gain, final_shift)
    result, backward = jax.vjp(forward, *inputs)
    grads = backward(cotangent.astype(jnp.float32))
    return (result.astype(jnp.bfloat16), grads[0], grads[1], grads[2], grads[3], grads[4], grads[5], grads[6], grads[7], grads[8], grads[9], grads[10], grads[11], grads[12], grads[13], grads[14], grads[15], grads[16], grads[17], grads[18])
```

```python
import math

import jax
import jax.numpy as jnp
from jax import lax
from jax.sharding import PartitionSpec as P

HEADS = 8
SLOT = 64


epsilon = 1e-05
masked_score = -1e30


def silu_slope(values):
    sigma = jax.nn.sigmoid(values)
    return sigma * (1.0 + values * (1.0 - sigma))


def graph_mask(sizes):
    return (jnp.arange(SLOT)[None, :] < sizes[:, None]).reshape(-1).astype(jnp.float32)


def blank_like(params):
    return tuple((jnp.zeros(item.shape, jnp.float32) for item in params))


def gine_forward(states, bonds, edge_table, weight_one, bias_one, weight_two):
    floats = states.astype(jnp.float32)
    kinds = edge_table.shape[0]
    graphs = bonds.shape[0]
    width = states.shape[1]
    shifted = floats[None] + edge_table[:, None, :]
    sent = jax.nn.silu(shifted).astype(jnp.bfloat16)
    onehot = (bonds[None] == (1 + jnp.arange(kinds))[:, None, None, None]).astype(jnp.bfloat16)
    message = jnp.einsum(
        "tgij,tgjd->gid",
        onehot,
        sent.reshape(kinds, graphs, SLOT, width),
        preferred_element_type=jnp.float32,
    ).reshape(-1, width)
    joined = (floats + message).astype(jnp.bfloat16)
    gine_first = jnp.dot(joined, weight_one, preferred_element_type=jnp.float32) + bias_one
    gine_act = jax.nn.silu(gine_first).astype(jnp.bfloat16)
    gine_last = jnp.dot(gine_act, weight_two, preferred_element_type=jnp.float32)
    return (gine_last + floats, (shifted, onehot, joined, gine_first, gine_act))


def gine_backward(grad_pre, states, bonds, edge_table, weight_one, bias_one, weight_two):
    unused, saved = gine_forward(states, bonds, edge_table, weight_one, bias_one, weight_two)
    shifted, onehot, joined, gine_first, gine_act = saved
    kinds = edge_table.shape[0]
    graphs = bonds.shape[0]
    width = states.shape[1]
    two_in = grad_pre.astype(jnp.bfloat16)
    weight_two_grad = jnp.einsum("rd,re->de", gine_act, two_in, preferred_element_type=jnp.float32)
    act_grad = jnp.einsum("re,de->rd", two_in, weight_two, preferred_element_type=jnp.float32)
    one_in = (act_grad * silu_slope(gine_first)).astype(jnp.bfloat16)
    weight_one_grad = jnp.einsum("rd,re->de", joined, one_in, preferred_element_type=jnp.float32)
    bias_one_grad = jnp.sum(one_in.astype(jnp.float32), axis=0)
    joined_back = jnp.einsum("re,de->rd", one_in, weight_one, preferred_element_type=jnp.float32)
    message_grad = joined_back.astype(jnp.bfloat16).reshape(graphs, SLOT, width)
    sent_grad = jnp.einsum(
        "tgij,gid->tgjd", onehot, message_grad, preferred_element_type=jnp.float32
    ).reshape(kinds, -1, width)
    shifted_grad = sent_grad * silu_slope(shifted)
    table_grad = jnp.sum(shifted_grad, axis=1)
    grad_states = grad_pre + joined_back + jnp.sum(shifted_grad, axis=0)
    return (grad_states, (table_grad, weight_one_grad, bias_one_grad, weight_two_grad))


def attend_forward(states, present, query_weight, query_bias, key_weight, value_weight, out_weight):
    rows, width = states.shape
    graphs = rows // SLOT
    head_size = width // HEADS
    scaling = 1.0 / math.sqrt(head_size)
    query = (
        (jnp.dot(states, query_weight, preferred_element_type=jnp.float32) + query_bias)
        .astype(jnp.bfloat16)
        .reshape(graphs, SLOT, HEADS, head_size)
    )
    keys = (
        jnp.dot(states, key_weight, preferred_element_type=jnp.float32)
        .astype(jnp.bfloat16)
        .reshape(graphs, SLOT, HEADS, head_size)
    )
    values = (
        jnp.dot(states, value_weight, preferred_element_type=jnp.float32)
        .astype(jnp.bfloat16)
        .reshape(graphs, SLOT, HEADS, head_size)
    )
    live_keys = present.reshape(graphs, 1, 1, SLOT) > 0.5
    scores = (
        jnp.einsum("gihe,gjhe->ghij", query, keys, preferred_element_type=jnp.float32) * scaling
    )
    probs = jax.nn.softmax(jnp.where(live_keys, scores, masked_score), axis=-1)
    weights = probs.astype(jnp.bfloat16)
    mixed = (
        jnp.einsum("ghij,gjhe->gihe", weights, values, preferred_element_type=jnp.float32)
        .reshape(rows, width)
        .astype(jnp.bfloat16)
    )
    attn_out = jnp.dot(mixed, out_weight, preferred_element_type=jnp.float32)
    return (attn_out + states.astype(jnp.float32), (query, keys, values, probs, weights, mixed))


def attend_backward(
    grad_pre, states, present, query_weight, query_bias, key_weight, value_weight, out_weight
):
    unused, saved = attend_forward(
        states, present, query_weight, query_bias, key_weight, value_weight, out_weight
    )
    query, keys, values, probs, weights, mixed = saved
    rows, width = states.shape
    graphs = rows // SLOT
    head_size = width // HEADS
    scaling = 1.0 / math.sqrt(head_size)
    out_in = grad_pre.astype(jnp.bfloat16)
    out_weight_grad = jnp.einsum("rd,re->de", mixed, out_in, preferred_element_type=jnp.float32)
    mixed_grad = (
        jnp.einsum("re,de->rd", out_in, out_weight, preferred_element_type=jnp.float32)
        .astype(jnp.bfloat16)
        .reshape(graphs, SLOT, HEADS, head_size)
    )
    probs_grad = jnp.einsum(
        "gihe,gjhe->ghij", mixed_grad, values, preferred_element_type=jnp.float32
    )
    values_grad = (
        jnp.einsum("ghij,gihe->gjhe", weights, mixed_grad, preferred_element_type=jnp.float32)
        .reshape(rows, width)
        .astype(jnp.bfloat16)
    )
    score_grad = (
        probs * (probs_grad - jnp.sum(probs * probs_grad, axis=-1, keepdims=True))
    ).astype(jnp.bfloat16)
    query_grad = (
        (
            jnp.einsum("ghij,gjhe->gihe", score_grad, keys, preferred_element_type=jnp.float32)
            * scaling
        )
        .reshape(rows, width)
        .astype(jnp.bfloat16)
    )
    key_grad = (
        (
            jnp.einsum("ghij,gihe->gjhe", score_grad, query, preferred_element_type=jnp.float32)
            * scaling
        )
        .reshape(rows, width)
        .astype(jnp.bfloat16)
    )
    query_weight_grad = jnp.einsum(
        "rd,re->de", states, query_grad, preferred_element_type=jnp.float32
    )
    query_bias_grad = jnp.sum(query_grad.astype(jnp.float32), axis=0)
    key_weight_grad = jnp.einsum("rd,re->de", states, key_grad, preferred_element_type=jnp.float32)
    value_weight_grad = jnp.einsum(
        "rd,re->de", states, values_grad, preferred_element_type=jnp.float32
    )
    grad_states = grad_pre + jnp.einsum(
        "re,de->rd", query_grad, query_weight, preferred_element_type=jnp.float32
    )
    grad_states = grad_states + jnp.einsum(
        "re,de->rd", key_grad, key_weight, preferred_element_type=jnp.float32
    )
    grad_states = grad_states + jnp.einsum(
        "re,de->rd", values_grad, value_weight, preferred_element_type=jnp.float32
    )
    return (
        grad_states,
        (query_weight_grad, query_bias_grad, key_weight_grad, value_weight_grad, out_weight_grad),
    )


def norm_stats(values, present):
    count = jnp.sum(present)
    mean = jnp.sum(present * values, axis=0) / count
    offset = values - mean
    return (mean, jnp.sum(present * offset * offset, axis=0))


def body(
    node_states,
    cotangent,
    counts,
    bond_types,
    edge_table,
    gine_weight_one,
    gine_bias_one,
    gine_weight_two,
    gine_gain,
    gine_shift,
    query_weight,
    query_bias,
    key_weight,
    value_weight,
    out_weight,
    attn_gain,
    attn_shift,
    ffn_weight_up,
    ffn_bias_up,
    ffn_weight_down,
    final_gain,
    final_shift,
):
    axes = ("dp", "branch")
    side = lax.axis_index("branch")
    half = counts.shape[0] // 2
    own_counts = lax.dynamic_slice_in_dim(counts, side * half, half)
    own_bonds = lax.dynamic_slice_in_dim(bond_types, side * half, half)
    present = graph_mask(own_counts)[:, None]
    own_total = jnp.sum(present)
    gine_params = (edge_table, gine_weight_one, gine_bias_one, gine_weight_two)
    attn_params = (query_weight, query_bias, key_weight, value_weight, out_weight)
    gine_pre, _ = gine_forward(node_states, own_bonds, *gine_params)
    attn_pre, _ = attend_forward(node_states, present[:, 0], *attn_params)

    def merge(stats):
        means, squares, totals = lax.all_gather(stats, axes, axis=0)
        node_total = jnp.sum(totals)
        mean = jnp.sum(means * totals[:, None], axis=0) / node_total
        shift = means - mean
        square = jnp.sum(squares + totals[:, None] * shift * shift, axis=0)
        return mean, lax.rsqrt(square / node_total + epsilon), node_total

    both = jnp.concatenate([gine_pre, attn_pre], axis=1)
    mean, squares = norm_stats(both, present)
    mean, rstd, node_total = merge((mean, squares, own_total))
    gains = jnp.concatenate([gine_gain, attn_gain])
    shifts = jnp.concatenate([gine_shift, attn_shift])
    width = node_states.shape[1]
    hat = (both - mean) * rstd
    normed = present * (gains * hat + shifts)
    joined_h = normed[:, :width] + normed[:, width:]
    hidden_in = joined_h.astype(jnp.bfloat16)
    up_pre = jnp.dot(hidden_in, ffn_weight_up, preferred_element_type=jnp.float32) + ffn_bias_up
    up_act = jax.nn.silu(up_pre).astype(jnp.bfloat16)
    ffn_pre = joined_h + jnp.dot(up_act, ffn_weight_down, preferred_element_type=jnp.float32)
    final_mean, final_squares = norm_stats(ffn_pre, present)
    final_mean, final_rstd, _ = merge((final_mean, final_squares, own_total))
    final_hat = (ffn_pre - final_mean) * final_rstd
    layer_output = (present * (final_gain * final_hat + final_shift)).astype(jnp.bfloat16)
    out_grad = present * cotangent.astype(jnp.float32)
    final_shift_grad, final_gain_grad = lax.psum(
        (jnp.sum(out_grad, axis=0), jnp.sum(out_grad * final_hat, axis=0)), axes
    )
    grad_y = (
        present
        * final_gain
        * final_rstd
        * (out_grad - final_shift_grad / node_total - final_hat * final_gain_grad / node_total)
    )
    down_in = grad_y.astype(jnp.bfloat16)
    down_grad = jnp.einsum("rf,rd->fd", up_act, down_in, preferred_element_type=jnp.float32)
    up_in = (
        jnp.einsum("rd,fd->rf", down_in, ffn_weight_down, preferred_element_type=jnp.float32)
        * silu_slope(up_pre)
    ).astype(jnp.bfloat16)
    up_grad = jnp.einsum("rd,rf->df", hidden_in, up_in, preferred_element_type=jnp.float32)
    up_bias_grad = jnp.sum(up_in.astype(jnp.float32), axis=0)
    joined_grad = present * (
        grad_y + jnp.einsum("rf,df->rd", up_in, ffn_weight_up, preferred_element_type=jnp.float32)
    ).astype(jnp.bfloat16).astype(jnp.float32)
    twice = jnp.concatenate([joined_grad, joined_grad], axis=1)
    shift_grads, gain_grads = lax.psum(
        (jnp.sum(twice, axis=0), jnp.sum(twice * hat, axis=0)), axes
    )
    pre_grads = present * gains * rstd * (
        twice - shift_grads / node_total - hat * gain_grads / node_total
    )
    gine_states, gine_grads = gine_backward(
        pre_grads[:, :width], node_states, own_bonds, *gine_params
    )
    attn_states, attn_grads = attend_backward(
        pre_grads[:, width:], node_states, present[:, 0], *attn_params
    )
    node_grads = gine_states + attn_states
    table, one, bias_one, two, query, query_b, key, value, out, up, up_b, down = lax.psum(
        (*gine_grads, *attn_grads, up_grad, up_bias_grad, down_grad), axes
    )
    return (
        layer_output,
        node_grads,
        table,
        one,
        bias_one,
        two,
        gain_grads[:width],
        shift_grads[:width],
        query,
        query_b,
        key,
        value,
        out,
        gain_grads[width:],
        shift_grads[width:],
        up,
        up_b,
        down,
        final_gain_grad,
        final_shift_grad,
    )


def solution(mesh):
    placed = (
        P(("dp", "branch"), None),
        P(("dp", "branch"), None),
        P("dp"),
        P("dp", None, None),
        P(),
        P(),
        P(),
        P(),
        P(),
        P(),
        P(),
        P(),
        P(),
        P(),
        P(),
        P(),
        P(),
        P(),
        P(),
        P(),
        P(),
        P(),
    )
    return jax.shard_map(
        body,
        mesh=mesh,
        in_specs=placed,
        out_specs=(
            P(("dp", "branch"), None),
            P(("dp", "branch"), None),
            P(),
            P(),
            P(),
            P(),
            P(),
            P(),
            P(),
            P(),
            P(),
            P(),
            P(),
            P(),
            P(),
            P(),
            P(),
            P(),
            P(),
            P(),
        ),
        check_vma=False,
    )
```

```python
import functools
import math

import jax
import jax.numpy as jnp
from jax import lax
from jax.experimental import pallas as pl
from jax.experimental.pallas import tpu as pltpu
from jax.sharding import PartitionSpec as P

HEADS = 8
SLOT = 64
HALF = 128
PAIR = 2 * SLOT
GROUP = 4 * SLOT
EPSILON = 1e-05
MASKED = -1e30
MESH = pl.DeviceIdType.MESH
F32 = jnp.float32
BF16 = jnp.bfloat16


def dot(left, right):
    return jnp.dot(left, right, preferred_element_type=F32)


def dot_nt(left, right):
    return lax.dot_general(left, right, (((1,), (1,)), ((), ())), preferred_element_type=F32)


def dot_tn(left, right):
    return lax.dot_general(left, right, (((0,), (0,)), ((), ())), preferred_element_type=F32)


def sigmoid(values):
    return 0.5 * jnp.tanh(0.5 * values) + 0.5


def silu_and_slope(values):
    sigma = sigmoid(values)
    act = values * sigma
    return act, sigma + act * (1.0 - sigma)


def column_sum(values):
    return jnp.sum(values, axis=0, keepdims=True)


def twice(values):
    return jnp.concatenate([values, values], axis=1)


def put_rows(ref, index, first, vectors):
    row = first
    for vector in vectors:
        for at in range(0, vector.shape[1], HALF):
            ref[index, row : row + 1, :] = vector[:, at : at + HALF]
            row += 1


def kernel(
    dp,
    states,
    cotangent,
    counts,
    bonds,
    table,
    w1,
    b1,
    w2,
    gine_gain,
    gine_shift,
    wq,
    bq,
    wk,
    wv,
    wo,
    attn_gain,
    attn_shift,
    wup,
    bup,
    wdn,
    final_gain,
    final_shift,
    o_layer,
    o_nodes,
    o_table,
    o_w1,
    o_b1,
    o_w2,
    o_gine_gain,
    o_gine_shift,
    o_wq,
    o_bq,
    o_wk,
    o_wv,
    o_wo,
    o_attn_gain,
    o_attn_shift,
    o_wup,
    o_bup,
    o_wdn,
    o_final_gain,
    o_final_shift,
    present,
    pad,
    hot,
    slopes,
    joined,
    act,
    slope_one,
    gine_pre,
    q_s,
    k_s,
    v_s,
    probs,
    mixed,
    attn_pre,
    hidden,
    up_act,
    up_slope,
    y_s,
    down_in,
    up_in,
    jg_s,
    two_in,
    out_in,
    one_in,
    dq_s,
    dk_s,
    dv_s,
    stat_a,
    stat_b,
    stat_c,
    stat_d,
    part,
    core_in,
    half_sum,
    rs_in,
    hi_in,
    gathered,
    sem_stat_s,
    sem_stat_r,
    sem_s,
    sem_r,
):
    rows, width = states.shape
    kinds = table.shape[0]
    groups = rows // GROUP
    mols = rows // SLOT
    devices = 2 * dp
    ring = min(dp, 16)
    outer = dp // ring
    share = width // ring
    my_dp = lax.axis_index("dp")
    core = lax.axis_index("branch")
    flat = 2 * my_dp + core
    low = my_dp % ring
    high = my_dp // ring

    def device_of(place):
        return (place // 2, place % 2)

    barrier = pltpu.get_barrier_semaphore()

    def greet(k, carry):
        pl.semaphore_signal(
            barrier, inc=1, device_id=device_of((flat + k) % devices), device_id_type=MESH
        )
        return carry

    lax.fori_loop(1, devices, greet, 0)

    def round_start(ref, which, height):
        def one(k, carry):
            pltpu.make_async_remote_copy(
                src_ref=ref.at[flat, pl.ds(0, height)],
                dst_ref=ref.at[flat, pl.ds(0, height)],
                send_sem=sem_stat_s.at[which],
                recv_sem=sem_stat_r.at[which],
                device_id=device_of((flat + k) % devices),
                device_id_type=MESH,
            ).start()
            return carry

        lax.fori_loop(1, devices, one, 0)

    def round_wait(ref, which, height):
        view = ref.at[pl.ds(0, devices - 1), pl.ds(0, height)]
        pltpu.make_async_copy(view, view, sem_stat_s.at[which]).wait()
        pltpu.make_async_copy(view, view, sem_stat_r.at[which]).wait()

    def sets(which):
        return ((0, 4), (4, 3), (7, 3))[which]

    def remote(src, dst, slot, target):
        return pltpu.make_async_remote_copy(
            src_ref=src,
            dst_ref=dst,
            send_sem=sem_s.at[slot],
            recv_sem=sem_r.at[slot],
            device_id=target,
            device_id_type=MESH,
        )

    def core_start(which):
        first, many = sets(which)
        remote(
            part.at[1 - core, pl.ds(first, many)],
            core_in.at[pl.ds(first, many)],
            5 * which,
            (my_dp, 1 - core),
        ).start()

    def wait_both(view, slot):
        pltpu.make_async_copy(view, view, sem_s.at[slot]).wait()
        pltpu.make_async_copy(view, view, sem_r.at[slot]).wait()

    def core_finish(which):
        first, many = sets(which)
        wait_both(core_in.at[pl.ds(first, many)], 5 * which)
        for block in range(first, first + many):
            half_sum[block] = (
                part[core, block].astype(F32) + core_in[block].astype(F32)
            ).astype(BF16)

        def one(k, carry):
            target = (low + k) % ring
            remote(
                half_sum.at[pl.ds(first, many), pl.ds(target * share, share)],
                rs_in.at[low, pl.ds(first, many)],
                5 * which + 1,
                (high * ring + target, core),
            ).start()
            return carry

        lax.fori_loop(1, ring, one, 0)
        rs_in[low, first : first + many] = half_sum[
            first : first + many, pl.ds(low * share, share), :
        ]

    def ring_finish(which):
        first, many = sets(which)
        if ring > 1:
            wait_both(rs_in.at[pl.ds(0, ring - 1), pl.ds(first, many)], 5 * which + 1)
        total = jnp.sum(rs_in[:, first : first + many].astype(F32), axis=0)
        if outer > 1:
            hi_in[high, first : first + many] = total.astype(BF16)

            def across(k, carry):
                target = (high + k) % outer
                remote(
                    hi_in.at[high, pl.ds(first, many)],
                    hi_in.at[high, pl.ds(first, many)],
                    5 * which + 2,
                    (target * ring + low, core),
                ).start()
                return carry

            lax.fori_loop(1, outer, across, 0)
            wait_both(hi_in.at[pl.ds(0, outer - 1), pl.ds(first, many)], 5 * which + 2)
            total = jnp.sum(hi_in[:, first : first + many].astype(F32), axis=0)
        own = pl.ds(low * share, share)
        gathered[core, first : first + many, own, :] = total.astype(BF16)

        def one(k, carry):
            piece = gathered.at[core, pl.ds(first, many), own]
            remote(
                piece, piece, 5 * which + 3, (high * ring + (low + k) % ring, core)
            ).start()
            return carry

        lax.fori_loop(1, ring, one, 0)

    def gather_finish(which):
        first, many = sets(which)
        if ring > 1:
            wait_both(
                gathered.at[0, pl.ds(first, many), pl.ds(0, (ring - 1) * share)], 5 * which + 3
            )
        mine = gathered.at[core, pl.ds(first, many)]
        remote(mine, mine, 5 * which + 4, (my_dp, 1 - core)).start()

    def whole_finish(which):
        first, many = sets(which)
        wait_both(gathered.at[0, pl.ds(first, many)], 5 * which + 4)

    def put_part(block, grad):
        part[0, block] = grad[:, :HALF].astype(BF16)
        part[1, block] = grad[:, HALF:].astype(BF16)

    def read_whole(block):
        return jnp.concatenate([gathered[0, block], gathered[1, block]], axis=1).astype(F32)

    pad[...] = jnp.zeros_like(pad)
    own_total = jnp.zeros((), F32)
    for m in range(mols):
        count = counts[core * mols + m]
        own_total = own_total + count.astype(F32)
        slot = lax.broadcasted_iota(jnp.int32, (SLOT, HALF), 0)
        present[m * SLOT : (m + 1) * SLOT, :] = jnp.where(slot < count, 1.0, 0.0)
    own_inverse = 1.0 / jnp.full((1, width), own_total, F32)
    top = lax.broadcasted_iota(jnp.int32, (PAIR, HALF), 0) < SLOT
    left = lax.broadcasted_iota(jnp.int32, (1, HALF), 1) < SLOT
    lane = lax.broadcasted_iota(jnp.int32, (SLOT, HALF), 1)
    key_slot = lax.broadcasted_iota(jnp.int32, (SLOT, HALF), 0)
    head_size = width // HEADS
    per_half = HALF // head_size
    scaling = 1.0 / math.sqrt(head_size)
    to_two = scaling * math.log2(math.e)
    zero16 = jnp.zeros((PAIR, HALF), BF16)

    def spread(value):
        return jnp.concatenate(
            [jnp.where(top, value, zero16), jnp.where(top, zero16, value)], axis=1
        )

    def by_head(value):
        blocks = []
        for h in range(per_half):
            inside = (lane >= h * head_size) & (lane < (h + 1) * head_size)
            blocks.append(
                jnp.concatenate(
                    [
                        jnp.where(inside, value[:SLOT], zero16[:SLOT]),
                        jnp.where(inside, value[SLOT:], zero16[:SLOT]),
                    ],
                    axis=1,
                )
            )
        return jnp.concatenate(blocks, axis=0)

    def pick_rows(value):
        return jnp.where(top, value[:, :HALF], value[:, HALF:])

    def pick_heads(value):
        parts = []
        for side in range(2):
            total = jnp.zeros((SLOT, HALF), F32)
            for h in range(per_half):
                inside = (lane >= h * head_size) & (lane < (h + 1) * head_size)
                block = value[h * SLOT : (h + 1) * SLOT, side * HALF : (side + 1) * HALF]
                total = jnp.where(inside, block, total)
            parts.append(total)
        return jnp.concatenate(parts, axis=0)

    def forward(g, sums):
        at = pl.ds(pl.multiple_of(g * GROUP, GROUP), GROUP)
        x = states[at, :]
        xf = x.astype(F32)
        q_s[at, :] = (dot(x, wq[...]) + bq[...]).astype(BF16)
        k_s[at, :] = dot(x, wk[...]).astype(BF16)
        v_s[at, :] = dot(x, wv[...]).astype(BF16)
        for p in range(2):
            pair = 2 * g + p
            rows_at = pl.ds(pl.multiple_of(g * GROUP + p * PAIR, PAIR), PAIR)
            mol = core * mols + 2 * pair
            pad[0:SLOT, 0:SLOT] = bonds[mol]
            pad[SLOT:PAIR, SLOT:PAIR] = bonds[mol + 1]
            kind = pad[...]
            xp = xf[p * PAIR : (p + 1) * PAIR]
            hots, sents = [], []
            for t in range(kinds):
                one = jnp.where(kind == t + 1, 1.0, 0.0).astype(BF16)
                hot[pair, t] = one
                sent, slope = silu_and_slope(xp + table[t : t + 1, :])
                slopes[pair, t] = slope.astype(BF16)
                hots.append(one)
                sents.append(sent.astype(BF16))
            message = dot(jnp.concatenate(hots, axis=1), jnp.concatenate(sents, axis=0))
            joined[rows_at, :] = (xp + message).astype(BF16)
        first, slope = silu_and_slope(dot(joined[at, :], w1[...]) + b1[...])
        slope_one[at, :] = slope.astype(BF16)
        first = first.astype(BF16)
        act[at, :] = first
        live = twice(present[at, :])
        pre = dot(first, w2[...]) + xf
        gine_pre[at, :] = pre
        sum_gine = sums[0] + column_sum(live * pre)
        for p in range(2):
            pair = 2 * g + p
            rows_at = pl.ds(pl.multiple_of(g * GROUP + p * PAIR, PAIR), PAIR)
            mol = core * mols + 2 * pair
            alive = key_slot < jnp.where(left, counts[mol], counts[mol + 1])
            for side in range(2):
                cols = slice(side * HALF, (side + 1) * HALF)
                scores = dot_nt(by_head(k_s[rows_at, cols]), spread(q_s[rows_at, cols]))
                scores = scores.reshape(per_half, SLOT, HALF)
                scores = jnp.where(alive[None], scores, MASKED)
                peak = jnp.max(scores, axis=1, keepdims=True)
                powers = jnp.exp2((scores - peak) * to_two)
                weights = powers * (1.0 / jnp.sum(powers, axis=1, keepdims=True))
                weights = weights.reshape(per_half * SLOT, HALF).astype(BF16)
                probs[pair, side] = weights
                mixed[rows_at, cols] = pick_rows(
                    dot_tn(weights, by_head(v_s[rows_at, cols]))
                ).astype(BF16)
        pre = dot(mixed[at, :], wo[...]) + xf
        attn_pre[at, :] = pre
        return (sum_gine, sums[1] + column_sum(live * pre))

    nothing = jnp.zeros((1, width), F32)
    sum_gine, sum_attn = lax.fori_loop(0, groups, forward, (nothing, nothing))
    mean_gine, mean_attn = sum_gine * own_inverse, sum_attn * own_inverse

    def squares(g, sums):
        at = pl.ds(pl.multiple_of(g * GROUP, GROUP), GROUP)
        live = twice(present[at, :])
        one, two = live * (gine_pre[at, :] - mean_gine), live * (attn_pre[at, :] - mean_attn)
        return (sums[0] + column_sum(one * one), sums[1] + column_sum(two * two))

    square_gine, square_attn = lax.fori_loop(0, groups, squares, (nothing, nothing))
    put_rows(stat_a, flat, 0, (mean_gine, mean_attn, square_gine, square_attn))
    stat_a[flat, 8:9, :] = jnp.full((1, HALF), own_total, F32)
    pl.semaphore_wait(barrier, devices - 1)
    round_start(stat_a, 0, 9)

    def merged(ref, many):
        count = stat_a[:, 8:9, :]
        node_total = jnp.sum(count, axis=0)
        means = ref[:, 0:many, :]
        mean = jnp.sum(means * count, axis=0) / node_total
        offset = means - mean[None]
        square = jnp.sum(ref[:, many : 2 * many, :] + count * offset * offset, axis=0)
        return mean, lax.rsqrt(square / node_total + EPSILON), node_total

    def vector(value, row):
        return jnp.concatenate([value[row : row + 1], value[row + 1 : row + 2]], axis=1)

    round_wait(stat_a, 0, 9)
    mean, rstd, node_total = merged(stat_a, 4)
    inverse = twice(1.0 / node_total)
    mean_gine, mean_attn = vector(mean, 0), vector(mean, 2)
    rstd_gine, rstd_attn = vector(rstd, 0), vector(rstd, 2)
    scale_gine = gine_gain[...] * rstd_gine
    scale_attn = attn_gain[...] * rstd_attn

    def feed(g, sums):
        at = pl.ds(pl.multiple_of(g * GROUP, GROUP), GROUP)
        live = twice(present[at, :])
        h = live * (
            scale_gine * (gine_pre[at, :] - mean_gine)
            + gine_shift[...]
            + scale_attn * (attn_pre[at, :] - mean_attn)
            + attn_shift[...]
        )
        h16 = h.astype(BF16)
        hidden[at, :] = h16
        value, slope = silu_and_slope(dot(h16, wup[...]) + bup[...])
        value = value.astype(BF16)
        up_act[at, :] = value
        up_slope[at, :] = slope.astype(BF16)
        y = h + dot(value, wdn[...])
        y_s[at, :] = y
        return (
            sums[0] + column_sum(live * y),
            sums[1] + column_sum(live * cotangent[at, :].astype(F32)),
        )

    sum_y, sum_c = lax.fori_loop(0, groups, feed, (nothing, nothing))
    mean_y = sum_y * own_inverse

    def spread_y(g, sums):
        at = pl.ds(pl.multiple_of(g * GROUP, GROUP), GROUP)
        live = twice(present[at, :])
        offset = live * (y_s[at, :] - mean_y)
        return (
            sums[0] + column_sum(offset * offset),
            sums[1] + column_sum(offset * cotangent[at, :].astype(F32)),
        )

    square_y, cross_y = lax.fori_loop(0, groups, spread_y, (nothing, nothing))
    put_rows(stat_b, flat, 0, (mean_y, square_y, sum_c, cross_y))
    round_start(stat_b, 1, 8)
    round_wait(stat_b, 1, 8)
    mean, rstd, _ = merged(stat_b, 2)
    moved = stat_b[:, 0:2, :] - mean[None]
    c_total = jnp.sum(stat_b[:, 4:6, :], axis=0)
    c_gain = jnp.sum(stat_b[:, 6:8, :] + moved * stat_b[:, 4:6, :], axis=0) * rstd
    mean_y, rstd_y = vector(mean, 0), vector(rstd, 0)
    c_shift, c_gain = vector(c_total, 0), vector(c_gain, 0)
    o_final_shift[...] = c_shift
    o_final_gain[...] = c_gain

    scale_y = final_gain[...] * rstd_y
    shift_part, gain_part = c_shift * inverse, c_gain * inverse

    def feed_back(g, sums):
        at = pl.ds(pl.multiple_of(g * GROUP, GROUP), GROUP)
        live = twice(present[at, :])
        hat = (y_s[at, :] - mean_y) * rstd_y
        o_layer[at, :] = (live * (final_gain[...] * hat + final_shift[...])).astype(BF16)
        grad = (live * scale_y) * (cotangent[at, :].astype(F32) - shift_part - hat * gain_part)
        grad16 = grad.astype(BF16)
        down_in[at, :] = grad16
        inner = (dot_nt(grad16, wdn[...]) * up_slope[at, :].astype(F32)).astype(BF16)
        up_in[at, :] = inner
        back = (grad + dot_nt(inner, wup[...])).astype(BF16)
        jg_s[at, :] = back
        back = back.astype(F32)
        return (
            sums[0] + column_sum(back),
            sums[1] + column_sum(back * (gine_pre[at, :] - mean_gine)),
            sums[2] + column_sum(back * (attn_pre[at, :] - mean_attn)),
            sums[3] + column_sum(inner.astype(F32)),
        )

    wide = jnp.zeros((1, wup.shape[1]), F32)
    sum_j, cross_gine, cross_attn, sum_up = lax.fori_loop(
        0, groups, feed_back, (nothing, nothing, nothing, wide)
    )
    put_rows(stat_c, flat, 0, (sum_j, cross_gine * rstd_gine, cross_attn * rstd_attn, sum_up))
    round_start(stat_c, 2, 10)

    up_grad = dot_tn(hidden[...], up_in[...])
    put_part(0, up_grad[:, :width])
    put_part(1, up_grad[:, width:])
    for at in range(2):
        put_part(2 + at, dot_tn(up_act[:, at * width : (at + 1) * width], down_in[...]))
    core_start(0)

    round_wait(stat_c, 2, 10)
    sums = jnp.sum(stat_c[:, 0:10, :], axis=0)
    shift_sum, gain_gine, gain_attn = vector(sums, 0), vector(sums, 2), vector(sums, 4)
    o_gine_shift[...] = shift_sum
    o_attn_shift[...] = shift_sum
    o_gine_gain[...] = gain_gine
    o_attn_gain[...] = gain_attn
    o_bup[...] = jnp.concatenate([vector(sums, 6), vector(sums, 8)], axis=1)
    core_finish(0)

    shift_part = shift_sum * inverse
    gine_part, attn_part = gain_gine * inverse * rstd_gine, gain_attn * inverse * rstd_attn

    def back_one(g, sums):
        at = pl.ds(pl.multiple_of(g * GROUP, GROUP), GROUP)
        live = twice(present[at, :])
        base = jg_s[at, :].astype(F32) - shift_part
        one = (live * scale_gine) * (base - (gine_pre[at, :] - mean_gine) * gine_part)
        two = (live * scale_attn) * (base - (attn_pre[at, :] - mean_attn) * attn_part)
        o_nodes[at, :] = one + two
        one = one.astype(BF16)
        two_in[at, :] = one
        out_in[at, :] = two.astype(BF16)
        inner = (dot_nt(one, w2[...]) * slope_one[at, :].astype(F32)).astype(BF16)
        one_in[at, :] = inner
        return sums + column_sum(inner.astype(F32))

    sum_one = lax.fori_loop(0, groups, back_one, nothing)
    put_part(4, dot_tn(act[...], two_in[...]))
    put_part(5, dot_tn(mixed[...], out_in[...]))
    put_part(6, dot_tn(joined[...], one_in[...]))
    core_start(1)
    ring_finish(0)

    def back_attend(g, sums):
        at = pl.ds(pl.multiple_of(g * GROUP, GROUP), GROUP)
        mixed_grad = dot_nt(out_in[at, :], wo[...]).astype(BF16)
        for p in range(2):
            pair = 2 * g + p
            rows_at = pl.ds(pl.multiple_of(g * GROUP + p * PAIR, PAIR), PAIR)
            for side in range(2):
                cols = slice(side * HALF, (side + 1) * HALF)
                grad = spread(mixed_grad[p * PAIR : (p + 1) * PAIR, cols])
                weights = probs[pair, side]
                probs_grad = dot_nt(by_head(v_s[rows_at, cols]), grad)
                dv_s[rows_at, cols] = pick_heads(dot(weights, grad)).astype(BF16)
                soft = weights.astype(F32).reshape(per_half, SLOT, HALF)
                probs_grad = probs_grad.reshape(per_half, SLOT, HALF)
                inner = jnp.sum(soft * probs_grad, axis=1, keepdims=True)
                score_grad = (soft * (probs_grad - inner)).astype(BF16)
                score_grad = score_grad.reshape(per_half * SLOT, HALF)
                dk_s[rows_at, cols] = (
                    pick_heads(dot(score_grad, spread(q_s[rows_at, cols]))) * scaling
                ).astype(BF16)
                dq_s[rows_at, cols] = (
                    pick_rows(dot_tn(score_grad, by_head(k_s[rows_at, cols]))) * scaling
                ).astype(BF16)
        return sums + column_sum(dq_s[at, :].astype(F32))

    sum_q = lax.fori_loop(0, groups, back_attend, nothing)
    put_part(7, dot_tn(states[...], dq_s[...]))
    put_part(8, dot_tn(states[...], dk_s[...]))
    put_part(9, dot_tn(states[...], dv_s[...]))
    core_start(2)
    core_finish(1)
    gather_finish(0)

    def back_nodes(g, sums):
        at = pl.ds(pl.multiple_of(g * GROUP, GROUP), GROUP)
        joined_back = dot_nt(one_in[at, :], w1[...])
        message_grad = joined_back.astype(BF16)
        pieces = []
        for p in range(2):
            pair = 2 * g + p
            sent_grad = dot(
                hot[pair].reshape(kinds * PAIR, PAIR), message_grad[p * PAIR : (p + 1) * PAIR]
            )
            piece = joined_back[p * PAIR : (p + 1) * PAIR]
            for t in range(kinds):
                shifted = sent_grad[t * PAIR : (t + 1) * PAIR] * slopes[pair, t].astype(F32)
                piece = piece + shifted
                sums = sums[:t] + (sums[t] + column_sum(shifted),) + sums[t + 1 :]
            pieces.append(piece)
        o_nodes[at, :] += (
            jnp.concatenate(pieces, axis=0)
            + dot_nt(dq_s[at, :], wq[...])
            + dot_nt(dk_s[at, :], wk[...])
            + dot_nt(dv_s[at, :], wv[...])
        )
        return sums

    table_sums = lax.fori_loop(0, groups, back_nodes, (nothing,) * kinds)
    put_rows(stat_d, flat, 0, (sum_one, sum_q) + table_sums)
    height = 4 + 2 * kinds
    round_start(stat_d, 3, height)

    core_finish(2)
    ring_finish(1)
    ring_finish(2)
    whole_finish(0)
    o_wup[...] = jnp.concatenate([read_whole(0), read_whole(1)], axis=1)
    o_wdn[...] = jnp.concatenate([read_whole(2), read_whole(3)], axis=0)
    gather_finish(1)
    gather_finish(2)
    round_wait(stat_d, 3, height)
    sums = jnp.sum(stat_d[:, 0:height, :], axis=0)
    o_b1[...] = vector(sums, 0)
    o_bq[...] = vector(sums, 2)
    for t in range(kinds):
        o_table[t : t + 1, :] = vector(sums, 4 + 2 * t)
    whole_finish(1)
    o_w2[...] = read_whole(4)
    o_wo[...] = read_whole(5)
    o_w1[...] = read_whole(6)
    whole_finish(2)
    o_wq[...] = read_whole(7)
    o_wk[...] = read_whole(8)
    o_wv[...] = read_whole(9)


def layer(dp, *arrays):
    states, cotangent, counts, bonds, table, *rest = arrays
    rows, width = states.shape
    kinds = table.shape[0]
    inner = arrays[17].shape[1]
    pairs = rows // PAIR
    devices = 2 * dp
    ring = min(dp, 16)
    share = width // ring
    blocks = 10
    flat = [item.reshape(1, -1) if item.ndim == 1 else item for item in rest]

    def row(size):
        return jax.ShapeDtypeStruct((1, size), F32)

    def square(*shape):
        return jax.ShapeDtypeStruct(shape, F32)

    big = square(width, width)
    out_shape = (
        jax.ShapeDtypeStruct((rows, width), BF16),
        square(rows, width),
        square(kinds, width),
        big,
        row(width),
        big,
        row(width),
        row(width),
        big,
        row(width),
        big,
        big,
        big,
        row(width),
        row(width),
        square(width, inner),
        row(inner),
        square(inner, width),
        row(width),
        row(width),
    )

    def half_rows(columns=width):
        return pltpu.VMEM((rows, columns), BF16)

    def full_rows(columns=width):
        return pltpu.VMEM((rows, columns), F32)

    scratch = [
        full_rows(HALF),
        pltpu.VMEM((PAIR, PAIR), jnp.int32),
        pltpu.VMEM((pairs, kinds, PAIR, PAIR), BF16),
        pltpu.VMEM((pairs, kinds, PAIR, width), BF16),
        half_rows(),
        half_rows(),
        half_rows(),
        full_rows(),
        half_rows(),
        half_rows(),
        half_rows(),
        pltpu.VMEM((pairs, 2, 4 * SLOT, HALF), BF16),
        half_rows(),
        full_rows(),
        half_rows(),
        half_rows(inner),
        half_rows(inner),
        full_rows(),
        half_rows(),
        half_rows(inner),
        half_rows(),
        half_rows(),
        half_rows(),
        half_rows(),
        half_rows(),
        half_rows(),
        half_rows(),
        pltpu.VMEM((devices, 16, HALF), F32),
        pltpu.VMEM((devices, 8, HALF), F32),
        pltpu.VMEM((devices, 16, HALF), F32),
        pltpu.VMEM((devices, 16, HALF), F32),
        pltpu.VMEM((2, blocks, width, HALF), BF16),
        pltpu.VMEM((blocks, width, HALF), BF16),
        pltpu.VMEM((blocks, width, HALF), BF16),
        pltpu.VMEM((ring, blocks, share, HALF), BF16),
        pltpu.VMEM((dp // ring, blocks, share, HALF), BF16),
        pltpu.VMEM((2, blocks, width, HALF), BF16),
        pltpu.SemaphoreType.DMA((4,)),
        pltpu.SemaphoreType.DMA((4,)),
        pltpu.SemaphoreType.DMA((15,)),
        pltpu.SemaphoreType.DMA((15,)),
    ]
    vmem = pl.BlockSpec(memory_space=pltpu.VMEM)
    in_specs = [vmem] * len(arrays)
    in_specs[2] = pl.BlockSpec(memory_space=pltpu.SMEM)
    outs = pl.pallas_call(
        functools.partial(kernel, dp),
        out_shape=out_shape,
        in_specs=in_specs,
        out_specs=(vmem,) * len(out_shape),
        scratch_shapes=scratch,
        compiler_params=pltpu.CompilerParams(
            collective_id=0, has_side_effects=True, vmem_limit_bytes=60 * 1024 * 1024
        ),
        name="layer",
    )(states, cotangent, counts, bonds, table, *flat)
    flat_places = (4, 6, 7, 9, 13, 14, 16, 18, 19)
    return tuple(item[0] if i in flat_places else item for i, item in enumerate(outs))


def solution(mesh):
    rows, whole = P(("dp", "branch"), None), P()
    placed = (rows, rows, P("dp"), P("dp", None, None)) + (whole,) * 18
    return jax.shard_map(
        functools.partial(layer, mesh.shape["dp"]),
        mesh=mesh,
        in_specs=placed,
        out_specs=(rows, rows) + (whole,) * 18,
        check_vma=False,
    )
```
